32 devices in a mesh: group: 2 (over y), tm: 16 (over z, x, core), height: 1.
Axes of the slice: x: 2, y: 2, z: 4, core: 2. Of those that a mesh axis runs over, the one named last changes fastest.
Arguments:
- query: bfloat16 [32, 2, 64, 1536], P(('group', 'tm'), 'height'), parts along dimension 0
- cur_kv: bfloat16 [2, 32, 2, 64, 1536], P(None, ('group', 'tm'), 'height'), parts along dimension 1
- cur_pos: int32 [3, 32, 2, 64], P(None, ('group', 'tm'), 'height'), parts along dimension 1, may hold values from 0 to 63
- cache_kv: bfloat16 [32, 2, 32, 1536], P(('group', 'tm'), None, 'height'), parts along dimension 0
- cache_pos: int32 [32, 3, 32], P(('group', 'tm'), None, 'height'), parts along dimension 0, may hold values from 0 to 63
- counts: int32 [32, 1], P(('group', 'tm'), 'height'), parts along dimension 0, may hold values from 1 to 32
- visible: int32 [32, 16], P(('group', 'tm')), parts along dimension 0, may hold values 0 or 1
Outputs:
- attended: bfloat16 [32, 2, 64, 1536], P(('group', 'tm'), 'height'), parts along dimension 0
The draws below stay inside these ranges and needn't reach their ends.
There are 2 independent parts, one for each index of `group`. The reference program is written for one: setup_inputs(seed, part) draws one part's arguments, and reference() takes and returns one part's arrays. A program takes and returns all parts, laid end to end along the dimension named above; each array names one. Nothing has to cross between parts.
Inputs may be any that keep to these rules, and one draw needn't show every extreme that they name: `counts`: every earlier span has at least one live slot in each row tile.
All inputs are finite; a program needn't handle non-finite values. No bound on the sum of `visible` on one device may be relied on, other than what follows from the above.
Results may differ from the reference program's by a relative error of at most 0.006.
The reference program's roundings to bfloat16 on the way count: a program that leaves them out, or rounds other values in their place, can miss the bound.
Values may be sent and summed in bfloat16 or wider, within the bound.
No kernel may reach another device: no remote copies, remote signals or barrier semaphores. Data moves between devices by JAX's collectives and lax.ppermute only.
A program may use at most 64 MiB of HBM per device.

```python
import jax
import jax.numpy as jnp
from jax import lax

HEADS = 12
HEAD = 128
ROWS_DEV = 2
WID = 64
CTOK = 32
REACH = 2
NROWS = 2
SPAN_FR = 16
CACHED = 16
HT_TOK = 32
N_HEIGHT = 1


def draw_tokens(key, shape):
    base = jnp.clip(jax.random.normal(key, shape, jnp.float32), -4.0, 4.0)
    return base.astype(jnp.bfloat16)


def draw_query(key, part):
    return draw_tokens(jax.random.fold_in(key, 11), (SPAN_FR, NROWS, WID, HEADS * HEAD))


def draw_cur_kv(key, part):
    return draw_tokens(jax.random.fold_in(key, 13), (2, SPAN_FR, NROWS, WID, HEADS * HEAD))


def draw_cache_kv(key, part):
    return draw_tokens(jax.random.fold_in(key, 17), (CACHED, 2, HT_TOK, HEADS * HEAD))


def plant(drawn, rng, least, largest):
    spot = [jax.random.randint(jax.random.fold_in(rng, axis), (), 0, length) for axis, length in enumerate(drawn.shape)]
    widest = drawn.shape.index(max(drawn.shape))
    beside = spot[:widest] + [(spot[widest] + 1) % drawn.shape[widest]] + spot[widest + 1:]
    return drawn.at[tuple(spot)].set(least).at[tuple(beside)].set(largest)


def setup_inputs(seed: int = 0, part: int = 0) -> dict:
    arg_keys = jax.random.split(jax.random.key(seed), 8)
    part_keys = jax.random.split(jax.random.fold_in(arg_keys[7], part), 8)
    return {
        "query": draw_query(jax.random.fold_in(jax.random.fold_in(arg_keys[7], part), 71), part),
        "cur_kv": draw_cur_kv(jax.random.fold_in(jax.random.fold_in(arg_keys[7], part), 71), part),
        "cur_pos": plant(jax.random.randint(part_keys[2], (3, SPAN_FR, NROWS, WID), 0, 64), jax.random.fold_in(part_keys[2], 1), 0, 63).astype(jnp.int32),
        "cache_kv": draw_cache_kv(jax.random.fold_in(jax.random.fold_in(arg_keys[7], part), 71), part),
        "cache_pos": plant(jax.random.randint(part_keys[4], (CACHED, 3, HT_TOK), 0, 64), jax.random.fold_in(part_keys[4], 1), 0, 63).astype(jnp.int32),
        "counts": plant(jax.random.randint(part_keys[5], (CACHED, N_HEIGHT), 1, CTOK + 1), jax.random.fold_in(part_keys[5], 1), 1, CTOK).astype(jnp.int32),
        "visible": plant((jax.random.randint(part_keys[6], (SPAN_FR, CACHED), 0, 4) < 3).astype(jnp.int32), jax.random.fold_in(part_keys[6], 1), 0, 1),
    }


def rope_tables():
    half = HEAD // 2
    index = jnp.arange(half)
    first = HEAD // 8
    second = 3 * HEAD // 16
    member = (index >= first).astype(jnp.int32) + (index >= first + second).astype(jnp.int32)
    begin = jnp.where(member == 0, 0, jnp.where(member == 1, first, first + second))
    length = jnp.where(member == 0, first, jnp.where(member == 1, second, half - first - second))
    frequency = jnp.power(10000.0, -(index - begin).astype(jnp.float32) / length.astype(jnp.float32))
    select = (member[None, :] == jnp.arange(3)[:, None]).astype(jnp.float32) * frequency[None, :]
    return select


def rotate(vectors, pos_time, pos_row, pos_column):
    select = rope_tables()
    angle = (pos_time.astype(jnp.float32)[..., None] * select[0]
             + pos_row.astype(jnp.float32)[..., None] * select[1]
             + pos_column.astype(jnp.float32)[..., None] * select[2])
    cosine = jnp.cos(angle)[..., None, :]
    sine = jnp.sin(angle)[..., None, :]
    shaped = vectors.astype(jnp.float32).reshape(vectors.shape[:-1] + (HEADS, 2, HEAD // 2))
    lower = shaped[..., 0, :]
    upper = shaped[..., 1, :]
    turned = jnp.stack([lower * cosine - upper * sine, upper * cosine + lower * sine], axis=-2)
    return turned.reshape(vectors.shape).astype(jnp.bfloat16)


def reference(query, cur_kv, cur_pos, cache_kv, cache_pos, counts, visible):
    depth = HEADS * HEAD
    scale = HEAD ** -0.5
    q_rot = rotate(query, cur_pos[0], cur_pos[1], cur_pos[2])
    k_rot = rotate(cur_kv[0], cur_pos[0], cur_pos[1], cur_pos[2])
    c_rot = rotate(cache_kv[:, 0], cache_pos[:, 0], cache_pos[:, 1], cache_pos[:, 2])
    c_values = cache_kv[:, 1]
    zero_rows = jnp.zeros((SPAN_FR, REACH, WID, depth), jnp.bfloat16)
    k_padded = jnp.concatenate([zero_rows, k_rot, zero_rows], axis=1)
    v_padded = jnp.concatenate([zero_rows, cur_kv[1], zero_rows], axis=1)
    extent = ROWS_DEV + 2 * REACH
    queries = ROWS_DEV * WID

    def one_tile(number):
        frame = (number // N_HEIGHT).astype(jnp.int32)
        tile_row = (number % N_HEIGHT).astype(jnp.int32)
        first_row = tile_row * ROWS_DEV
        zero = jnp.zeros((), jnp.int32)
        q_tile = lax.dynamic_slice(q_rot, (frame, first_row, zero, zero), (1, ROWS_DEV, WID, depth)).reshape(queries, HEADS, HEAD)
        k_tile = lax.dynamic_slice(k_padded, (frame, first_row, zero, zero), (1, extent, WID, depth)).reshape(extent * WID, HEADS, HEAD)
        v_tile = lax.dynamic_slice(v_padded, (frame, first_row, zero, zero), (1, extent, WID, depth)).reshape(extent * WID, HEADS, HEAD)
        c_keys = lax.dynamic_slice(c_rot, (zero, tile_row * CTOK, zero), (CACHED, CTOK, depth)).reshape(CACHED * CTOK, HEADS, HEAD)
        c_vals = lax.dynamic_slice(c_values, (zero, tile_row * CTOK, zero), (CACHED, CTOK, depth)).reshape(CACHED * CTOK, HEADS, HEAD)
        all_keys = jnp.concatenate([k_tile, c_keys], axis=0)
        all_values = jnp.concatenate([v_tile, c_vals], axis=0)
        query_row = first_row + jnp.arange(queries) // WID
        key_row = first_row - REACH + jnp.arange(extent * WID) // WID
        local_ok = ((key_row[None, :] >= 0) & (key_row[None, :] < NROWS)
                    & (jnp.abs(query_row[:, None] - key_row[None, :]) <= REACH))
        live = lax.dynamic_slice(counts, (zero, tile_row), (CACHED, 1))[:, 0]
        seen = lax.dynamic_slice(visible, (frame, zero), (1, CACHED))[0]
        cache_ok = ((seen[:, None] > 0) & (jnp.arange(CTOK)[None, :] < live[:, None])).reshape(CACHED * CTOK)
        allowed = jnp.concatenate([local_ok, jnp.broadcast_to(cache_ok[None, :], (queries, CACHED * CTOK))], axis=1)
        scores = jnp.einsum("qhd,khd->qhk", q_tile.astype(jnp.float32), all_keys.astype(jnp.float32)) * scale
        scores = jnp.where(allowed[:, None, :], scores, -jnp.inf)
        highest = jnp.max(scores, axis=-1, keepdims=True)
        weights = jnp.where(allowed[:, None, :], jnp.exp(scores - highest), 0.0)
        totals = jnp.sum(weights, axis=-1)
        rounded = lax.optimization_barrier(weights.astype(jnp.bfloat16))
        summed = jnp.einsum("qhk,khd->qhd", rounded.astype(jnp.float32), all_values.astype(jnp.float32))
        return (summed / totals[..., None]).astype(jnp.bfloat16).reshape(ROWS_DEV, WID, depth)

    tiles = lax.map(one_tile, jnp.arange(SPAN_FR * N_HEIGHT))
    return tiles.reshape(SPAN_FR, NROWS, WID, depth)
```

```python
import functools

import jax
import jax.numpy as jnp
import numpy as np
from jax import lax
from jax.experimental import pallas as pl
from jax.experimental.pallas import tpu as pltpu
from jax.sharding import PartitionSpec as P

HEADS = 12
HEAD = 128
REACH = 2
EXP_SCALE = HEAD**-0.5 * 1.4426950408889634


def rope_rows():
    half = HEAD // 2
    first = HEAD // 8
    second = 3 * HEAD // 16
    rows = np.zeros((8, HEAD), np.float32)
    groups = ((0, first), (first, second), (first + second, half - first - second))
    for group, (begin, length) in enumerate(groups):
        exponent = -np.arange(length, dtype=np.float32) / np.float32(length)
        rows[group, begin : begin + length] = np.power(np.float32(10000.0), exponent)
    rows[:, half:] = rows[:, :half]
    rows[3, :half] = -1.0
    rows[3, half:] = 1.0
    return rows


def tables(positions, rows):
    turned = positions.T
    angle = (
        turned[:, 0:1] * rows[0:1] + turned[:, 1:2] * rows[1:2] + turned[:, 2:3] * rows[2:3]
    )
    return jnp.cos(angle), jnp.sin(angle) * rows[3:4]


def turn(vectors, cosine, sine):
    wide = vectors.astype(jnp.float32)
    return wide * cosine + pltpu.roll(wide, HEAD // 2, 1) * sine


def columns(head):
    return slice(head * HEAD, (head + 1) * HEAD)


def product(left, right, contract):
    return lax.dot_general(
        left, right, (((1,), (contract,)), ((), ())), preferred_element_type=jnp.float32
    )


def spread(value, width):
    copies = -(-width // HEAD)
    if copies == 1:
        return value[:, :width]
    return jnp.concatenate([value] * copies, axis=1)[:, :width]


def pack_kernel(kv_ref, pos_ref, count_ref, rows_ref, out_ref, pos_scratch):
    slots = kv_ref.shape[2]
    pos_scratch[...] = jnp.zeros_like(pos_scratch)
    pos_scratch[0:3, 0:slots] = pos_ref[0].astype(jnp.float32)
    cosine, sine = tables(pos_scratch[...], rows_ref[...])
    cosine, sine = cosine[:slots], sine[:slots]
    slot = lax.broadcasted_iota(jnp.int32, (slots, HEAD), 0)
    lane = lax.broadcasted_iota(jnp.int32, (slots, HEAD), 1)
    live = slot < count_ref[0, 0]
    mark = jnp.where(lane == 0, jnp.inf, 0.0)
    for head in range(HEADS):
        turned = turn(kv_ref[0, 0, :, columns(head)], cosine, sine)
        turned = jnp.where(live, turned, mark if head == 0 else 0.0)
        out_ref[0:slots, columns(head)] = turned.astype(jnp.bfloat16)
    out_ref[slots:, :] = kv_ref[0, 1]


def local_kernel(
    masked, q_ref, kv_ref, pos_ref, rows_ref, rot_ref, high_ref, total_ref, sum_ref, pos_scratch
):
    tile_rows, wide = q_ref.shape[1], q_ref.shape[2]
    extent = kv_ref.shape[2]
    queries, keys = tile_rows * wide, extent * wide
    reach = (extent - tile_rows) // 2
    pos_scratch[...] = jnp.zeros_like(pos_scratch)
    for row in range(extent):
        for group in range(3):
            pos_scratch[group : group + 1, row * wide : (row + 1) * wide] = pos_ref[
                group, 0, row : row + 1, :
            ].astype(jnp.float32)
    cosine, sine = tables(pos_scratch[...], rows_ref[...])
    begin = reach * wide
    q_cosine, q_sine = cosine[begin : begin + queries], sine[begin : begin + queries]
    if masked:
        tile = lax.axis_index("height")
        count = lax.axis_size("height")
        query_row = lax.broadcasted_iota(jnp.int32, (queries, keys), 0) // wide
        key_row = lax.broadcasted_iota(jnp.int32, (queries, keys), 1) // wide - reach
        first = tile * tile_rows
        allowed = (
            (key_row + first >= 0)
            & (key_row + first < tile_rows * count)
            & (jnp.abs(query_row - key_row) <= REACH)
        )
        cap = jnp.where(allowed, jnp.inf, -jnp.inf)
    for head in range(HEADS):
        part = columns(head)
        query = turn(q_ref[0, :, :, part].reshape(queries, HEAD), q_cosine, q_sine)
        query = query.astype(jnp.bfloat16)
        rot_ref[:, part] = query
        key = turn(kv_ref[0, 0, :, :, part].reshape(keys, HEAD), cosine, sine)
        scores = product(query, key.astype(jnp.bfloat16), 1)
        if masked:
            scores = jnp.minimum(scores, cap)
        high = jnp.max(scores, axis=1, keepdims=True)
        weights = jnp.exp2((scores - high) * EXP_SCALE)
        total = jnp.sum(weights, axis=1, keepdims=True)
        value = kv_ref[1, 0, :, :, part].reshape(keys, HEAD)
        sum_ref[:, part] = product(weights.astype(jnp.bfloat16), value, 0)
        high_ref[:, part] = jnp.broadcast_to(high, (queries, HEAD))
        total_ref[:, part] = jnp.broadcast_to(total, (queries, HEAD))


def source(offset_own, cross, pairs):
    me = lax.axis_index("tm")
    core = lax.rem(me, 2)
    column = lax.rem(me // 2, 2)
    line = me // 4
    place = jnp.where(column == 0, line, pairs - 1 - line)
    step = jnp.where(core == 0, offset_own, -offset_own)
    there = lax.rem(place - step + 2 * pairs, pairs)
    half = pairs // 2
    far = there >= half
    line = jnp.where(far, pairs - 1 - there, there)
    column = jnp.where(far, 1, 0)
    return line * 4 + column * 2 + (1 - core if cross else core)


def block_kernel(order, pairs, final, *refs):
    count = len(order)
    rot_ref, high_ref, total_ref, sum_ref, seen_ref = refs[:5]
    blocks = refs[5 : 5 + count]
    outs = refs[5 + count :]
    slots = blocks[0].shape[0] // 2
    keys = count * slots
    queries = rot_ref.shape[0]
    place = lax.broadcasted_iota(jnp.int32, (8, keys), 1) // slots
    seen = jnp.zeros((8, keys), jnp.int32)
    for number, (offset, cross) in enumerate(order):
        shown = seen_ref[0, source(offset, cross, pairs)]
        seen = jnp.where(place == number, shown, seen)

    def gathered(part, begin):
        return jnp.concatenate([block[begin : begin + slots, part] for block in blocks], axis=0)

    first = gathered(columns(0), 0)
    lane = lax.broadcasted_iota(jnp.int32, (8, HEAD), 1)
    pick = jnp.where(lane == 0, 1.0, 0.0).astype(jnp.bfloat16)
    marks = product(pick, first, 1)
    cap = jnp.where((marks < jnp.inf) & (seen > 0), jnp.inf, -jnp.inf)[0:1]
    cap = jnp.broadcast_to(cap, (queries, keys))
    for head in range(HEADS):
        part = columns(head)
        key = gathered(part, 0)
        if head == 0:
            key = jnp.where(key == jnp.inf, jnp.zeros_like(key), key)
        scores = jnp.minimum(product(rot_ref[:, part], key, 1), cap)
        before = high_ref[:, part]
        high = jnp.maximum(before, jnp.max(scores, axis=1, keepdims=True))
        weights = jnp.exp2((scores - spread(high, keys)) * EXP_SCALE)
        fading = jnp.exp2((before - high) * EXP_SCALE)
        total = total_ref[:, part] * fading + jnp.sum(weights, axis=1, keepdims=True)
        added = product(weights.astype(jnp.bfloat16), gathered(part, slots), 0)
        summed = sum_ref[:, part] * fading + added
        if final:
            out_ref = outs[0]
            result = (summed / total).astype(jnp.bfloat16)
            out_ref[0, :, :, part] = result.reshape(out_ref.shape[1], out_ref.shape[2], HEAD)
        else:
            outs[0][:, part] = high
            outs[1][:, part] = total
            outs[2][:, part] = summed


VMEM = pl.BlockSpec(memory_space=pltpu.VMEM)
SMEM = pl.BlockSpec(memory_space=pltpu.SMEM)
PARAMS = pltpu.CompilerParams(vmem_limit_bytes=40 * 1024 * 1024)


def cost(flops, size, special):
    return pl.CostEstimate(flops=flops, bytes_accessed=size, transcendentals=special)


def pack(cache_kv, cache_pos, counts, rows):
    slots, depth = cache_kv.shape[2:]
    return pl.pallas_call(
        pack_kernel,
        out_shape=jax.ShapeDtypeStruct((2 * slots, depth), jnp.bfloat16),
        in_specs=[VMEM, VMEM, SMEM, VMEM],
        out_specs=VMEM,
        scratch_shapes=[pltpu.VMEM((8, 128), jnp.float32)],
        compiler_params=PARAMS,
        name="pack",
    )(cache_kv, cache_pos, counts, rows)


def local_attention(query, pair, pos, rows, masked):
    tile_rows, wide, depth = query.shape[1:]
    queries, keys = tile_rows * wide, pair.shape[2] * wide
    state = jax.ShapeDtypeStruct((queries, depth), jnp.float32)
    return pl.pallas_call(
        functools.partial(local_kernel, masked),
        out_shape=[jax.ShapeDtypeStruct((queries, depth), jnp.bfloat16), state, state, state],
        in_specs=[VMEM] * 4,
        out_specs=[VMEM] * 4,
        scratch_shapes=[pltpu.VMEM((8, keys), jnp.float32)],
        compiler_params=PARAMS,
        cost_estimate=cost(4 * queries * keys * depth, 4000000, queries * keys * HEADS),
        name="local_attention",
    )(query, pair, pos, rows)


def block_attention(rot, state, visible, blocks, order, pairs, out=None):
    queries, depth = rot.shape
    keys = len(blocks) * blocks[0].shape[0] // 2
    shape = jax.ShapeDtypeStruct((queries, depth), jnp.float32)
    return pl.pallas_call(
        functools.partial(block_kernel, order, pairs, out is not None),
        out_shape=[shape] * 3 if out is None else [out],
        in_specs=[VMEM] * 4 + [SMEM] + [VMEM] * len(blocks),
        out_specs=[VMEM] * (3 if out is None else 1),
        compiler_params=PARAMS,
        cost_estimate=cost(4 * queries * keys * depth, 4000000, queries * keys * HEADS),
        name="block_attention" if out is None else "last_attention",
    )(rot, *state, visible, *blocks)


def ring_moves(size):
    pairs = size // 2

    def place(index):
        line, column = index // 4, (index // 2) % 2
        return line if column == 0 else pairs - 1 - line

    def index_of(where, core):
        where %= pairs
        column = int(where >= pairs // 2)
        line = pairs - 1 - where if column else where
        return line * 4 + column * 2 + core

    return [
        (index, index_of(place(index) + (1 if index % 2 == 0 else -1), index % 2))
        for index in range(size)
    ]


def extended(cells, dim, width):
    count = lax.axis_size("height")
    ends = count - 1
    head = lax.slice_in_dim(cells, 0, width, axis=dim)
    tail = lax.slice_in_dim(cells, cells.shape[dim] - width, cells.shape[dim], axis=dim)
    above = lax.ppermute(tail, "height", [(i, i + 1) for i in range(ends)])
    below = lax.ppermute(head, "height", [(i + 1, i) for i in range(ends)])
    return jnp.concatenate([above, cells, below], axis=dim)


def per_device(query, cur_kv, cur_pos, cache_kv, cache_pos, counts, visible):
    size = lax.axis_size("tm")
    pairs = size // 2
    moves = ring_moves(size)
    swap = [(index, index ^ 1) for index in range(size)]

    def onward(block):
        return lax.ppermute(block, "tm", moves)

    def across(block):
        return lax.ppermute(block, "tm", swap)

    rows = jnp.asarray(rope_rows())
    own = pack(cache_kv, cache_pos, counts, rows)
    masked = lax.axis_size("height") > 1 or query.shape[1] - 1 > REACH
    if lax.axis_size("height") > 1:
        pair, pos = extended(cur_kv, 2, REACH), extended(cur_pos, 2, REACH)
    else:
        pair, pos = cur_kv, cur_pos
    rot, *state = local_attention(query, pair, pos, rows, masked)

    blocks = [own, across(own)]
    order = [(0, False), (0, True)]
    same, other = blocks
    half = pairs // 2
    for step in range(1, half + 1):
        same = onward(same)
        blocks += [same, across(same)]
        order += [(step, False), (-step, True)]
        if step < half:
            other = onward(other)
            blocks += [other, across(other)]
            order += [(step, True), (-step, False)]
    early = 2 + 4 * (half - 2)
    state = block_attention(rot, state, visible, blocks[:early], order[:early], pairs)
    out = jax.ShapeDtypeStruct(query.shape, jnp.bfloat16)
    return block_attention(rot, state, visible, blocks[early:], order[early:], pairs, out)[0]


def solution(mesh):
    in_specs = (
        P(("group", "tm"), "height", None, None),
        P(None, ("group", "tm"), "height", None, None),
        P(None, ("group", "tm"), "height", None),
        P(("group", "tm"), None, "height", None),
        P(("group", "tm"), None, "height"),
        P(("group", "tm"), "height"),
        P(("group", "tm"), None),
    )
    out_specs = P(("group", "tm"), "height", None, None)
    return jax.shard_map(
        per_device, mesh=mesh, in_specs=in_specs, out_specs=out_specs, check_vma=False
    )
```

```python
import functools

import jax
import jax.numpy as jnp
import numpy as np
from jax import lax
from jax.experimental import pallas as pl
from jax.experimental.pallas import tpu as pltpu
from jax.sharding import PartitionSpec as P

HEADS = 12
HEAD = 128
REACH = 2
EXP_SCALE = HEAD**-0.5 * 1.4426950408889634
MARGIN = 16.0


def rope_rows():
    half = HEAD // 2
    first = HEAD // 8
    second = 3 * HEAD // 16
    rows = np.zeros((8, HEAD), np.float32)
    groups = ((0, first), (first, second), (first + second, half - first - second))
    for group, (begin, length) in enumerate(groups):
        exponent = -np.arange(length, dtype=np.float32) / np.float32(length)
        rows[group, begin : begin + length] = np.power(np.float32(10000.0), exponent)
    rows[:, half:] = rows[:, :half]
    rows[3, :half] = -1.0
    rows[3, half:] = 1.0
    return rows


def tables(positions, rows):
    turned = positions.T
    angle = (
        turned[:, 0:1] * rows[0:1] + turned[:, 1:2] * rows[1:2] + turned[:, 2:3] * rows[2:3]
    )
    return jnp.cos(angle), jnp.sin(angle) * rows[3:4]


def turn(vectors, cosine, sine):
    wide = vectors.astype(jnp.float32)
    return wide * cosine + pltpu.roll(wide, HEAD // 2, 1) * sine


def columns(head):
    return slice(head * HEAD, (head + 1) * HEAD)


def product(left, right, contract):
    return lax.dot_general(
        left, right, (((1,), (contract,)), ((), ())), preferred_element_type=jnp.float32
    )


def spread(value, width):
    copies = -(-width // HEAD)
    if copies == 1:
        return value[:, :width]
    return jnp.concatenate([value] * copies, axis=1)[:, :width]


def pack_kernel(
    kv_ref, pos_ref, count, rows_ref, out_ref, kv, pos, rows, pos_scratch, sems
):
    slots = kv.shape[2]
    copies = [
        pltpu.make_async_copy(there, here, sems.at[number])
        for number, (there, here) in enumerate(
            ((kv_ref, kv), (pos_ref, pos), (rows_ref, rows))
        )
    ]
    for copy in copies:
        copy.start()
    pos_scratch[...] = jnp.zeros_like(pos_scratch)
    for copy in copies[::-1]:
        copy.wait()
    for group in range(3):
        pos_scratch[group : group + 1, 0:slots] = pos[group].astype(jnp.float32)
    cosine, sine = tables(pos_scratch[...], rows[...])
    cosine, sine = cosine[:slots], sine[:slots]
    slot = lax.broadcasted_iota(jnp.int32, (slots, HEAD), 0)
    lane = lax.broadcasted_iota(jnp.int32, (slots, HEAD), 1)
    live = slot < count[0, 0]
    mark = jnp.where(lane == 0, jnp.inf, 0.0)
    for head in range(HEADS):
        turned = turn(kv[0, 0, :, columns(head)], cosine, sine)
        turned = jnp.where(live, turned, mark if head == 0 else 0.0)
        out_ref[0:slots, columns(head)] = turned.astype(jnp.bfloat16)
    out_ref[slots:, :] = kv[0, 1]


def pipelined(count, first, second, third):
    waiting = second(0, first(0))
    ahead = first(1)
    for step in range(count):
        done = third(step, waiting)
        if step + 1 < count:
            waiting = second(step + 1, ahead)
        if step + 2 < count:
            ahead = first(step + 2)
        done()


def sums_of(weights, value):
    both = product(weights, jnp.concatenate([value, jnp.ones_like(value)], axis=1), 0)
    return both[:, :HEAD], both[:, HEAD:]


def local_kernel(masked, order, pairs, *refs):
    query_ref, pair_ref, place_ref, rows_ref, visible = refs[:5]
    rot_ref, shift_ref, total_ref, sum_ref, seen_ref = refs[5:10]
    q_ref, kv_ref, pos_ref, rows, pos_scratch, sems = refs[10:]
    copies = [
        pltpu.make_async_copy(there, here, sems.at[number])
        for number, (there, here) in enumerate(
            (
                (place_ref, pos_ref),
                (rows_ref, rows),
                (query_ref, q_ref),
                (pair_ref.at[0], kv_ref.at[0]),
                (pair_ref.at[1], kv_ref.at[1]),
            )
        )
    ]
    for copy in copies:
        copy.start()
    tile_rows, wide = q_ref.shape[1], q_ref.shape[2]
    extent = kv_ref.shape[2]
    queries, keys = tile_rows * wide, extent * wide
    reach = (extent - tile_rows) // 2
    pos_scratch[...] = jnp.zeros_like(pos_scratch)
    copies[0].wait()
    for row in range(extent):
        for group in range(3):
            pos_scratch[group : group + 1, row * wide : (row + 1) * wide] = pos_ref[
                group, 0, row : row + 1, :
            ].astype(jnp.float32)
    copies[1].wait()
    cosine, sine = tables(pos_scratch[...], rows[...])
    begin = reach * wide
    q_cosine, q_sine = cosine[begin : begin + queries], sine[begin : begin + queries]
    for copy in copies[2:]:
        copy.wait()
    slots = seen_ref.shape[1] // len(order)
    place = lax.broadcasted_iota(jnp.int32, seen_ref.shape, 1) // slots
    seen = jnp.zeros(seen_ref.shape, jnp.int32)
    for number, (offset, cross) in enumerate(order):
        seen = jnp.where(place == number, visible[0, source(offset, cross, pairs)], seen)
    seen_ref[...] = seen
    if masked:
        tile = lax.axis_index("height")
        count = lax.axis_size("height")
        query_row = lax.broadcasted_iota(jnp.int32, (queries, keys), 0) // wide
        key_row = lax.broadcasted_iota(jnp.int32, (queries, keys), 1) // wide - reach
        first = tile * tile_rows
        allowed = (
            (key_row + first >= 0)
            & (key_row + first < tile_rows * count)
            & (jnp.abs(query_row - key_row) <= REACH)
        )
        cap = jnp.where(allowed, jnp.inf, -jnp.inf)

    def score(head):
        part = columns(head)
        query = turn(q_ref[0, :, :, part].reshape(queries, HEAD), q_cosine, q_sine)
        query = query.astype(jnp.bfloat16)
        rot_ref[:, part] = query
        key = turn(kv_ref[0, 0, :, :, part].reshape(keys, HEAD), cosine, sine)
        scores = product(query, key.astype(jnp.bfloat16), 1)
        return jnp.minimum(scores, cap) if masked else scores

    def weight(head, scores):
        shift = jnp.max(scores, axis=1, keepdims=True) * EXP_SCALE + MARGIN
        shift_ref[:, columns(head)] = jnp.broadcast_to(shift, (queries, HEAD))
        return jnp.exp2(scores * EXP_SCALE - shift).astype(jnp.bfloat16)

    def apply(head, weights):
        part = columns(head)
        sums = sums_of(weights, kv_ref[1, 0, :, :, part].reshape(keys, HEAD))

        def store():
            sum_ref[:, part], total_ref[:, part] = sums

        return store

    pipelined(HEADS, score, weight, apply)


def source(offset_own, cross, pairs):
    me = lax.axis_index("tm")
    core = lax.rem(me, 2)
    column = lax.rem(me // 2, 2)
    line = me // 4
    place = jnp.where(column == 0, line, pairs - 1 - line)
    step = jnp.where(core == 0, offset_own, -offset_own)
    there = lax.rem(place - step + 2 * pairs, pairs)
    half = pairs // 2
    far = there >= half
    line = jnp.where(far, pairs - 1 - there, there)
    column = jnp.where(far, 1, 0)
    return line * 4 + column * 2 + (1 - core if cross else core)


def block_kernel(begin, final, *refs):
    rot_ref, shift_ref, total_ref, sum_ref, seen_ref = refs[:5]
    blocks, outs = (refs[5:-1], refs[-1:]) if final else (refs[5:-3], refs[-3:])
    slots = blocks[0].shape[0] // 2
    keys = len(blocks) * slots
    queries = rot_ref.shape[0]
    seen = seen_ref[:, begin * slots : begin * slots + keys]

    def gathered(part, begin):
        return jnp.concatenate([block[begin : begin + slots, part] for block in blocks], axis=0)

    lane = lax.broadcasted_iota(jnp.int32, (8, HEAD), 1)
    pick = jnp.where(lane == 0, 1.0, 0.0).astype(jnp.bfloat16)
    marks = product(pick, gathered(columns(0), 0), 1)
    cap = jnp.where((marks < jnp.inf) & (seen > 0), jnp.inf, -jnp.inf)[0:1]

    def score(part, clean):
        key = gathered(part, 0)
        if clean:
            key = jnp.where(key == jnp.inf, jnp.zeros_like(key), key)
        return jnp.minimum(product(rot_ref[:, part], key, 1), cap)

    def store(part, summed, total):
        if final:
            result = (summed / total).astype(jnp.bfloat16)
            outs[0][0, :, :, part] = result.reshape(outs[0].shape[1], outs[0].shape[2], HEAD)
        else:
            outs[1][:, part] = total
            outs[2][:, part] = summed

    top = [jnp.full((8, keys), -jnp.inf)]

    def weight(head, scores):
        power = scores * EXP_SCALE - spread(shift_ref[:, columns(head)], keys)
        top[0] = jnp.maximum(top[0], jnp.max(power.reshape(queries // 8, 8, keys), axis=0))
        return jnp.exp2(power).astype(jnp.bfloat16)

    def apply(head, weights):
        part = columns(head)
        summed, total = sums_of(weights, gathered(part, slots))
        return lambda: store(part, sum_ref[:, part] + summed, total_ref[:, part] + total)

    pipelined(HEADS, lambda head: score(columns(head), head == 0), weight, apply)

    @pl.when(jnp.max(top[0]) > 0.0)
    def _():
        @pl.loop(0, HEADS)
        def _(head):
            part = pl.ds(pl.multiple_of(head * HEAD, HEAD), HEAD)
            before = shift_ref[:, part]
            scores = score(part, True)
            shift = jnp.maximum(before, jnp.max(scores, axis=1, keepdims=True) * EXP_SCALE)
            fading = jnp.exp2(before - shift)
            weights = jnp.exp2(scores * EXP_SCALE - spread(shift, keys)).astype(jnp.bfloat16)
            summed, total = sums_of(weights, gathered(part, slots))
            store(part, sum_ref[:, part] * fading + summed, total_ref[:, part] * fading + total)
            if not final:
                outs[0][:, part] = shift


VMEM = pl.BlockSpec(memory_space=pltpu.VMEM)
SMEM = pl.BlockSpec(memory_space=pltpu.SMEM)
HBM = pl.BlockSpec(memory_space=pltpu.HBM)
PARAMS = pltpu.CompilerParams(vmem_limit_bytes=40 * 1024 * 1024)


def cost(flops, size, special):
    return pl.CostEstimate(flops=flops, bytes_accessed=size, transcendentals=special)


def in_place(array):
    return pltpu.with_memory_space_constraint(array, pltpu.HBM)


def pack(cache_kv, cache_pos, counts, rows):
    slots, depth = cache_kv.shape[2:]
    return pl.pallas_call(
        pack_kernel,
        out_shape=jax.ShapeDtypeStruct((2 * slots, depth), jnp.bfloat16),
        in_specs=[HBM, HBM, SMEM, HBM],
        out_specs=VMEM,
        scratch_shapes=[
            pltpu.VMEM(cache_kv.shape, cache_kv.dtype),
            pltpu.VMEM(cache_pos.shape, cache_pos.dtype),
            pltpu.VMEM(rows.shape, rows.dtype),
            pltpu.VMEM((8, 128), jnp.float32),
            pltpu.SemaphoreType.DMA((3,)),
        ],
        compiler_params=PARAMS,
        name="pack",
    )(in_place(cache_kv), in_place(cache_pos), counts, in_place(rows))


def local_attention(query, pair, pos, rows, visible, masked, order, pairs, slots):
    tile_rows, wide, depth = query.shape[1:]
    queries, keys = tile_rows * wide, pair.shape[2] * wide
    state = jax.ShapeDtypeStruct((queries, depth), jnp.float32)
    seen = jax.ShapeDtypeStruct((8, len(order) * slots), jnp.int32)
    inputs = (query, pair, pos, rows)
    return pl.pallas_call(
        functools.partial(local_kernel, masked, order, pairs),
        out_shape=[jax.ShapeDtypeStruct((queries, depth), jnp.bfloat16)] + [state] * 3 + [seen],
        in_specs=[HBM] * 4 + [SMEM],
        out_specs=[VMEM] * 5,
        scratch_shapes=[pltpu.VMEM(array.shape, array.dtype) for array in inputs]
        + [
            pltpu.VMEM((8, keys), jnp.float32),
            pltpu.SemaphoreType.DMA((5,)),
        ],
        compiler_params=PARAMS,
        cost_estimate=cost(4 * queries * keys * depth, 4000000, queries * keys * HEADS),
        name="local_attention",
    )(*[in_place(array) for array in inputs], visible)


def block_attention(rot, state, seen, blocks, begin, out=None):
    queries, depth = rot.shape
    keys = len(blocks) * blocks[0].shape[0] // 2
    final = out is not None
    shape = jax.ShapeDtypeStruct((queries, depth), jnp.float32)
    return pl.pallas_call(
        functools.partial(block_kernel, begin, final),
        out_shape=out if final else [shape] * 3,
        in_specs=[VMEM] * (5 + len(blocks)),
        out_specs=VMEM if final else [VMEM] * 3,
        input_output_aliases={} if final else {1: 0},
        compiler_params=PARAMS,
        cost_estimate=cost(4 * queries * keys * depth, 9000000, queries * keys * HEADS),
        name="last_attention" if final else "block_attention",
    )(rot, *state, seen, *blocks)


def ring_moves(size):
    pairs = size // 2

    def place(index):
        line, column = index // 4, (index // 2) % 2
        return line if column == 0 else pairs - 1 - line

    def index_of(where, core):
        where %= pairs
        column = int(where >= pairs // 2)
        line = pairs - 1 - where if column else where
        return line * 4 + column * 2 + core

    return [
        (index, index_of(place(index) + (1 if index % 2 == 0 else -1), index % 2))
        for index in range(size)
    ]


def extended(cells, dim, width):
    count = lax.axis_size("height")
    ends = count - 1
    head = lax.slice_in_dim(cells, 0, width, axis=dim)
    tail = lax.slice_in_dim(cells, cells.shape[dim] - width, cells.shape[dim], axis=dim)
    above = lax.ppermute(tail, "height", [(i, i + 1) for i in range(ends)])
    below = lax.ppermute(head, "height", [(i + 1, i) for i in range(ends)])
    return jnp.concatenate([above, cells, below], axis=dim)


def per_device(query, cur_kv, cur_pos, cache_kv, cache_pos, counts, visible):
    size = lax.axis_size("tm")
    pairs = size // 2
    moves = ring_moves(size)
    swap = [(index, index ^ 1) for index in range(size)]

    def onward(block):
        return lax.ppermute(block, "tm", moves)

    def across(block):
        return lax.ppermute(block, "tm", swap)

    rows = jnp.asarray(rope_rows())
    own = pack(cache_kv, jnp.swapaxes(cache_pos, 0, 1), counts, rows)
    masked = lax.axis_size("height") > 1 or query.shape[1] - 1 > REACH
    if lax.axis_size("height") > 1:
        pair, pos = extended(cur_kv, 2, REACH), extended(cur_pos, 2, REACH)
    else:
        pair, pos = cur_kv, cur_pos
    half = pairs // 2
    order = [(0, False), (0, True)]
    for step in range(1, half):
        order += [(step, False), (-step, True), (step, True), (-step, False)]
    order += [(half, False), (-half, True)]
    blocks = [own, across(own)]
    same, other = onward(blocks[0]), onward(blocks[1])
    rot, *state, seen = local_attention(
        query, pair, pos, rows, visible, masked, order, pairs, cache_kv.shape[2]
    )
    same, rot = lax.optimization_barrier((same, rot))
    for step in range(1, half):
        blocks += [same, across(same), other, across(other)]
        same = onward(same)
        if step + 1 < half:
            other = onward(other)
    last = [same, across(same)]
    state = block_attention(rot, state, seen, blocks, 0)
    out = jax.ShapeDtypeStruct(query.shape, jnp.bfloat16)
    return block_attention(rot, state, seen, last, len(blocks), out)


def solution(mesh):
    in_specs = (
        P(("group", "tm"), "height", None, None),
        P(None, ("group", "tm"), "height", None, None),
        P(None, ("group", "tm"), "height", None),
        P(("group", "tm"), None, "height", None),
        P(("group", "tm"), None, "height"),
        P(("group", "tm"), "height"),
        P(("group", "tm"), None),
    )
    out_specs = P(("group", "tm"), "height", None, None)
    return jax.shard_map(
        per_device, mesh=mesh, in_specs=in_specs, out_specs=out_specs, check_vma=False
    )
```

```python
import functools

import jax
import jax.numpy as jnp
import numpy as np
from jax import lax
from jax.experimental import pallas as pl
from jax.experimental.pallas import tpu as pltpu
from jax.sharding import PartitionSpec as P

HEADS = 12
HEAD = 128
REACH = 2
EXP_SCALE = HEAD**-0.5 * 1.4426950408889634
MARGIN = 16.0
BLOCK_GROUP = 6


def rope_rows():
    half = HEAD // 2
    first = HEAD // 8
    second = 3 * HEAD // 16
    rows = np.zeros((8, HEAD), np.float32)
    groups = ((0, first), (first, second), (first + second, half - first - second))
    for group, (begin, length) in enumerate(groups):
        exponent = -np.arange(length, dtype=np.float32) / np.float32(length)
        rows[group, begin : begin + length] = np.power(np.float32(10000.0), exponent)
    rows[:, half:] = rows[:, :half]
    rows[3, :half] = -1.0
    rows[3, half:] = 1.0
    return rows


def tables(positions, rows):
    turned = positions.T
    angle = (
        turned[:, 0:1] * rows[0:1] + turned[:, 1:2] * rows[1:2] + turned[:, 2:3] * rows[2:3]
    )
    return jnp.cos(angle), jnp.sin(angle) * rows[3:4]


def turn(vectors, cosine, sine):
    wide = vectors.astype(jnp.float32)
    return wide * cosine + pltpu.roll(wide, HEAD // 2, 1) * sine


def columns(head):
    return slice(head * HEAD, (head + 1) * HEAD)


def product(left, right, contract):
    return lax.dot_general(
        left, right, (((1,), (contract,)), ((), ())), preferred_element_type=jnp.float32
    )


def spread(value, width):
    copies = -(-width // HEAD)
    if copies == 1:
        return value[:, :width]
    return jnp.concatenate([value] * copies, axis=1)[:, :width]


def pack_kernel(
    kv_ref, pos_ref, count, rows_ref, out_ref, kv, pos, rows, pos_scratch, sems
):
    slots = kv.shape[0]
    copies = [
        pltpu.make_async_copy(there, here, sems.at[number])
        for number, (there, here) in enumerate(
            (
                (kv_ref.at[0, 0], kv),
                (pos_ref, pos),
                (rows_ref, rows),
                (kv_ref.at[0, 1], out_ref.at[slots:]),
            )
        )
    ]
    for copy in copies:
        copy.start()
    pos_scratch[...] = jnp.zeros_like(pos_scratch)
    for copy in copies[2::-1]:
        copy.wait()
    for group in range(3):
        pos_scratch[group : group + 1, 0:slots] = pos[group].astype(jnp.float32)
    cosine, sine = tables(pos_scratch[...], rows[...])
    cosine, sine = cosine[:slots], sine[:slots]
    slot = lax.broadcasted_iota(jnp.int32, (slots, HEAD), 0)
    lane = lax.broadcasted_iota(jnp.int32, (slots, HEAD), 1)
    live = slot < count[0, 0]
    mark = jnp.where(lane == 0, jnp.inf, 0.0)
    for head in range(HEADS):
        turned = turn(kv[:, columns(head)], cosine, sine)
        turned = jnp.where(live, turned, mark if head == 0 else 0.0)
        out_ref[0:slots, columns(head)] = turned.astype(jnp.bfloat16)
    copies[3].wait()


def staged(count, group, first, second, third):
    for base in range(0, count, group):
        steps = range(base, min(base + group, count))
        results = [first(step) for step in steps]
        results = [second(step, result) for step, result in zip(steps, results)]
        results = [third(step, result) for step, result in zip(steps, results)]
        for finish in results:
            finish()


def sums_of(weights, value):
    both = product(weights, jnp.concatenate([value, jnp.ones_like(value)], axis=1), 0)
    return both[:, :HEAD], both[:, HEAD:]


def turn_kernel(order, pairs, *refs):
    query_ref, pair_ref, place_ref, rows_ref, visible_ref = refs[:5]
    rot_ref, key_ref, value_ref, seen_ref = refs[5:9]
    q, k, positions, rows, visible, pos_scratch, sems = refs[9:]
    copies = [
        pltpu.make_async_copy(there, here, sems.at[number])
        for number, (there, here) in enumerate(
            (
                (place_ref, positions),
                (rows_ref, rows),
                (pair_ref.at[0], k),
                (query_ref, q),
                (visible_ref, visible),
                (pair_ref.at[1], value_ref),
            )
        )
    ]
    for copy in copies:
        copy.start()
    tile_rows, wide = q.shape[1], q.shape[2]
    extent = k.shape[1]
    queries, keys = tile_rows * wide, extent * wide
    begin = (extent - tile_rows) // 2 * wide
    pos_scratch[...] = jnp.zeros_like(pos_scratch)
    copies[0].wait()
    for row in range(extent):
        for group in range(3):
            pos_scratch[group : group + 1, row * wide : (row + 1) * wide] = positions[
                group, 0, row : row + 1, :
            ].astype(jnp.float32)
    copies[1].wait()
    cosine, sine = tables(pos_scratch[...], rows[...])
    copies[2].wait()
    for head in range(HEADS):
        part = columns(head)
        key = turn(k[0, :, :, part].reshape(keys, HEAD), cosine, sine)
        key_ref[:, part] = key.astype(jnp.bfloat16)
    cosine, sine = cosine[begin : begin + queries], sine[begin : begin + queries]
    copies[3].wait()
    for head in range(HEADS):
        part = columns(head)
        query = turn(q[0, :, :, part].reshape(queries, HEAD), cosine, sine)
        rot_ref[:, part] = query.astype(jnp.bfloat16)
    copies[4].wait()
    slots = seen_ref.shape[1] // len(order)
    place = lax.broadcasted_iota(jnp.int32, seen_ref.shape, 1) // slots
    seen = jnp.zeros(seen_ref.shape, jnp.int32)
    for number, (offset, cross) in enumerate(order):
        seen = jnp.where(place == number, visible[0, source(offset, cross, pairs)], seen)
    seen_ref[...] = seen
    copies[5].wait()


def local_kernel(masked, *refs):
    rot_ref, key_ref, value_ref, shift_ref, total_ref, sum_ref = refs
    extent, wide = value_ref.shape[1], value_ref.shape[2]
    queries, keys = rot_ref.shape[0], extent * wide
    tile_rows = queries // wide
    reach = (extent - tile_rows) // 2
    if masked:
        tile = lax.axis_index("height")
        count = lax.axis_size("height")
        query_row = lax.broadcasted_iota(jnp.int32, (queries, keys), 0) // wide
        key_row = lax.broadcasted_iota(jnp.int32, (queries, keys), 1) // wide - reach
        first = tile * tile_rows
        allowed = (
            (key_row + first >= 0)
            & (key_row + first < tile_rows * count)
            & (jnp.abs(query_row - key_row) <= REACH)
        )
        cap = jnp.where(allowed, jnp.inf, -jnp.inf)

    def score(head):
        part = columns(head)
        scores = product(rot_ref[:, part], key_ref[:, part], 1)
        return jnp.minimum(scores, cap) if masked else scores

    def weight(head, scores):
        shift = jnp.max(scores, axis=1, keepdims=True) * EXP_SCALE + MARGIN
        shift_ref[:, columns(head)] = jnp.broadcast_to(shift, (queries, HEAD))
        return jnp.exp2(scores * EXP_SCALE - shift).astype(jnp.bfloat16)

    def apply(head, weights):
        part = columns(head)
        sums = sums_of(weights, value_ref[0, :, :, part].reshape(keys, HEAD))

        def store():
            sum_ref[:, part], total_ref[:, part] = sums

        return store

    staged(HEADS, HEADS, score, weight, apply)


def source(offset_own, cross, pairs):
    me = lax.axis_index("tm")
    core = lax.rem(me, 2)
    column = lax.rem(me // 2, 2)
    line = me // 4
    place = jnp.where(column == 0, line, pairs - 1 - line)
    step = jnp.where(core == 0, offset_own, -offset_own)
    there = lax.rem(place - step + 2 * pairs, pairs)
    half = pairs // 2
    far = there >= half
    line = jnp.where(far, pairs - 1 - there, there)
    column = jnp.where(far, 1, 0)
    return line * 4 + column * 2 + (1 - core if cross else core)


def block_kernel(begin, final, *refs):
    rot_ref, shift_ref, total_ref, sum_ref, seen_ref = refs[:5]
    blocks, outs = (refs[5:-1], refs[-1:]) if final else (refs[5:-3], refs[-3:])
    slots = blocks[0].shape[0] // 2
    keys = len(blocks) * slots
    queries = rot_ref.shape[0]
    seen = seen_ref[:, begin * slots : begin * slots + keys]

    def gathered(part, begin):
        return jnp.concatenate([block[begin : begin + slots, part] for block in blocks], axis=0)

    lane = lax.broadcasted_iota(jnp.int32, (8, HEAD), 1)
    pick = jnp.where(lane == 0, 1.0, 0.0).astype(jnp.bfloat16)
    marks = product(pick, gathered(columns(0), 0), 1)
    cap = jnp.where((marks < jnp.inf) & (seen > 0), jnp.inf, -jnp.inf)[0:1]

    def score(part, clean):
        key = gathered(part, 0)
        if clean:
            key = jnp.where(key == jnp.inf, jnp.zeros_like(key), key)
        return jnp.minimum(product(rot_ref[:, part], key, 1), cap)

    def store(part, summed, total):
        if final:
            result = (summed / total).astype(jnp.bfloat16)
            outs[0][0, :, :, part] = result.reshape(outs[0].shape[1], outs[0].shape[2], HEAD)
        else:
            outs[1][:, part] = total
            outs[2][:, part] = summed

    top = [jnp.full((8, keys), -jnp.inf)]

    def weight(head, scores):
        power = scores * EXP_SCALE - spread(shift_ref[:, columns(head)], keys)
        top[0] = jnp.maximum(top[0], jnp.max(power.reshape(queries // 8, 8, keys), axis=0))
        return jnp.exp2(power).astype(jnp.bfloat16)

    def apply(head, weights):
        part = columns(head)
        summed, total = sums_of(weights, gathered(part, slots))
        return lambda: store(part, sum_ref[:, part] + summed, total_ref[:, part] + total)

    group = HEADS if final else BLOCK_GROUP
    staged(HEADS, group, lambda head: score(columns(head), head == 0), weight, apply)

    @pl.when(jnp.max(top[0]) > 0.0)
    def _():
        @pl.loop(0, HEADS)
        def _(head):
            part = pl.ds(pl.multiple_of(head * HEAD, HEAD), HEAD)
            before = shift_ref[:, part]
            scores = score(part, True)
            shift = jnp.maximum(before, jnp.max(scores, axis=1, keepdims=True) * EXP_SCALE)
            fading = jnp.exp2(before - shift)
            weights = jnp.exp2(scores * EXP_SCALE - spread(shift, keys)).astype(jnp.bfloat16)
            summed, total = sums_of(weights, gathered(part, slots))
            store(part, sum_ref[:, part] * fading + summed, total_ref[:, part] * fading + total)
            if not final:
                outs[0][:, part] = shift


VMEM = pl.BlockSpec(memory_space=pltpu.VMEM)
SMEM = pl.BlockSpec(memory_space=pltpu.SMEM)
HBM = pl.BlockSpec(memory_space=pltpu.HBM)
PARAMS = pltpu.CompilerParams(vmem_limit_bytes=40 * 1024 * 1024)


def cost(flops, size, special):
    return pl.CostEstimate(flops=flops, bytes_accessed=size, transcendentals=special)


def in_place(array):
    return pltpu.with_memory_space_constraint(array, pltpu.HBM)


def pack(cache_kv, cache_pos, counts, rows):
    slots, depth = cache_kv.shape[2:]
    return pl.pallas_call(
        pack_kernel,
        out_shape=jax.ShapeDtypeStruct((2 * slots, depth), jnp.bfloat16),
        in_specs=[HBM, HBM, SMEM, HBM],
        out_specs=VMEM,
        scratch_shapes=[
            pltpu.VMEM((slots, depth), cache_kv.dtype),
            pltpu.VMEM(cache_pos.shape, cache_pos.dtype),
            pltpu.VMEM(rows.shape, rows.dtype),
            pltpu.VMEM((8, 128), jnp.float32),
            pltpu.SemaphoreType.DMA((4,)),
        ],
        compiler_params=PARAMS,
        name="pack",
    )(in_place(cache_kv), in_place(cache_pos), counts, in_place(rows))


def turn_local(query, pair, pos, rows, visible, order, pairs, slots):
    depth = query.shape[-1]
    queries, keys = query.shape[1] * query.shape[2], pair.shape[2] * pair.shape[3]
    values = pair.shape[1:]
    return pl.pallas_call(
        functools.partial(turn_kernel, order, pairs),
        out_shape=[
            jax.ShapeDtypeStruct((queries, depth), jnp.bfloat16),
            jax.ShapeDtypeStruct((keys, depth), jnp.bfloat16),
            jax.ShapeDtypeStruct(values, jnp.bfloat16),
            jax.ShapeDtypeStruct((8, len(order) * slots), jnp.int32),
        ],
        in_specs=[HBM] * 5,
        out_specs=[VMEM] * 4,
        scratch_shapes=[
            pltpu.VMEM(query.shape, query.dtype),
            pltpu.VMEM(values, pair.dtype),
            pltpu.VMEM(pos.shape, pos.dtype),
            pltpu.VMEM(rows.shape, rows.dtype),
            pltpu.SMEM(visible.shape, visible.dtype),
            pltpu.VMEM((8, keys), jnp.float32),
            pltpu.SemaphoreType.DMA((6,)),
        ],
        compiler_params=PARAMS,
        cost_estimate=cost(0, 4000000, 0),
        name="turn_local",
    )(*[in_place(array) for array in (query, pair, pos, rows, visible)])


def local_attention(rot, key, value, masked):
    queries, depth = rot.shape
    keys = key.shape[0]
    state = jax.ShapeDtypeStruct((queries, depth), jnp.float32)
    return pl.pallas_call(
        functools.partial(local_kernel, masked),
        out_shape=[state] * 3,
        in_specs=[VMEM] * 3,
        out_specs=[VMEM] * 3,
        compiler_params=PARAMS,
        cost_estimate=cost(4 * queries * keys * depth, 4000000, queries * keys * HEADS),
        name="local_attention",
    )(rot, key, value)


def block_attention(rot, state, seen, blocks, begin, out=None):
    queries, depth = rot.shape
    keys = len(blocks) * blocks[0].shape[0] // 2
    final = out is not None
    shape = jax.ShapeDtypeStruct((queries, depth), jnp.float32)
    return pl.pallas_call(
        functools.partial(block_kernel, begin, final),
        out_shape=out if final else [shape] * 3,
        in_specs=[VMEM] * (5 + len(blocks)),
        out_specs=VMEM if final else [VMEM] * 3,
        input_output_aliases={} if final else {1: 0},
        compiler_params=PARAMS,
        cost_estimate=cost(4 * queries * keys * depth, 9000000, queries * keys * HEADS),
        name="last_attention" if final else "block_attention",
    )(rot, *state, seen, *blocks)


def ring_moves(size):
    pairs = size // 2

    def place(index):
        line, column = index // 4, (index // 2) % 2
        return line if column == 0 else pairs - 1 - line

    def index_of(where, core):
        where %= pairs
        column = int(where >= pairs // 2)
        line = pairs - 1 - where if column else where
        return line * 4 + column * 2 + core

    return [
        (index, index_of(place(index) + (1 if index % 2 == 0 else -1), index % 2))
        for index in range(size)
    ]


def extended(cells, dim, width):
    count = lax.axis_size("height")
    ends = count - 1
    head = lax.slice_in_dim(cells, 0, width, axis=dim)
    tail = lax.slice_in_dim(cells, cells.shape[dim] - width, cells.shape[dim], axis=dim)
    above = lax.ppermute(tail, "height", [(i, i + 1) for i in range(ends)])
    below = lax.ppermute(head, "height", [(i + 1, i) for i in range(ends)])
    return jnp.concatenate([above, cells, below], axis=dim)


def per_device(query, cur_kv, cur_pos, cache_kv, cache_pos, counts, visible):
    size = lax.axis_size("tm")
    pairs = size // 2
    moves = ring_moves(size)
    swap = [(index, index ^ 1) for index in range(size)]

    def onward(block):
        return lax.ppermute(block, "tm", moves)

    def across(block):
        return lax.ppermute(block, "tm", swap)

    rows = jnp.asarray(rope_rows())
    own = pack(cache_kv, jnp.swapaxes(cache_pos, 0, 1), counts, rows)
    masked = lax.axis_size("height") > 1 or query.shape[1] - 1 > REACH
    if lax.axis_size("height") > 1:
        pair, pos = extended(cur_kv, 2, REACH), extended(cur_pos, 2, REACH)
    else:
        pair, pos = cur_kv, cur_pos
    half = pairs // 2
    order = [(0, False), (0, True)]
    for step in range(1, half):
        order += [(step, False), (-step, True), (step, True), (-step, False)]
    order += [(half, False), (-half, True)]
    blocks = [own, across(own)]
    same, other = onward(blocks[0]), onward(blocks[1])
    rot, key, value, seen = turn_local(
        query, pair, pos, rows, visible, order, pairs, cache_kv.shape[2]
    )
    shift, *sums = local_attention(rot, key, value, masked)
    same, rot = lax.optimization_barrier((same, rot))
    for step in range(1, half):
        blocks += [same, across(same), other, across(other)]
        same = onward(same)
        if step == 1:
            same, shift = lax.optimization_barrier((same, shift))
        if step + 1 < half:
            other = onward(other)
    last = [same, across(same)]
    state = block_attention(rot, (shift, *sums), seen, blocks, 0)
    out = jax.ShapeDtypeStruct(query.shape, jnp.bfloat16)
    return block_attention(rot, state, seen, last, len(blocks), out)


def solution(mesh):
    in_specs = (
        P(("group", "tm"), "height", None, None),
        P(None, ("group", "tm"), "height", None, None),
        P(None, ("group", "tm"), "height", None),
        P(("group", "tm"), None, "height", None),
        P(("group", "tm"), None, "height"),
        P(("group", "tm"), "height"),
        P(("group", "tm"), None),
    )
    out_specs = P(("group", "tm"), "height", None, None)
    return jax.shard_map(
        per_device, mesh=mesh, in_specs=in_specs, out_specs=out_specs, check_vma=False
    )
```

```python
import functools

import jax
import jax.numpy as jnp
import numpy as np
from jax import lax
from jax.experimental import pallas as pl
from jax.experimental.pallas import tpu as pltpu
from jax.sharding import PartitionSpec as P

HEADS = 12
HEAD = 128
REACH = 2
EXP_SCALE = HEAD**-0.5 * 1.4426950408889634
MARGIN = 16.0
BLOCK_GROUP = 6


def rope_rows():
    half = HEAD // 2
    first = HEAD // 8
    second = 3 * HEAD // 16
    rows = np.zeros((8, HEAD), np.float32)
    groups = ((0, first), (first, second), (first + second, half - first - second))
    for group, (begin, length) in enumerate(groups):
        exponent = -np.arange(length, dtype=np.float32) / np.float32(length)
        rows[group, begin : begin + length] = np.power(np.float32(10000.0), exponent)
    rows[:, half:] = rows[:, :half]
    rows[3, :half] = -1.0
    rows[3, half:] = 1.0
    return rows


def rope_lanes():
    half = HEAD // 2
    first = HEAD // 8
    second = 3 * HEAD // 16
    group = lax.broadcasted_iota(jnp.int32, (8, HEAD), 0)
    lane = lax.broadcasted_iota(jnp.int32, (8, HEAD), 1)
    index = jnp.where(lane < half, lane, lane - half)
    member = (index >= first).astype(jnp.int32) + (index >= first + second).astype(jnp.int32)
    begin = jnp.where(member == 0, 0, jnp.where(member == 1, first, first + second))
    length = jnp.where(member == 0, first, jnp.where(member == 1, second, half - first - second))
    exponent = (index - begin).astype(jnp.float32) / length.astype(jnp.float32)
    frequency = jnp.exp(exponent * -9.210340371976184)
    sign = jnp.where(lane < half, -1.0, 1.0)
    return jnp.where(group == member, frequency, jnp.where(group == 3, sign, 0.0))


def tables(positions, rows):
    turned = positions.T
    angle = (
        turned[:, 0:1] * rows[0:1] + turned[:, 1:2] * rows[1:2] + turned[:, 2:3] * rows[2:3]
    )
    return jnp.cos(angle), jnp.sin(angle) * rows[3:4]


def turn(vectors, cosine, sine):
    wide = vectors.astype(jnp.float32)
    return wide * cosine + pltpu.roll(wide, HEAD // 2, 1) * sine


def columns(head):
    return slice(head * HEAD, (head + 1) * HEAD)


def product(left, right, contract):
    return lax.dot_general(
        left, right, (((1,), (contract,)), ((), ())), preferred_element_type=jnp.float32
    )


def spread(value, width):
    copies = -(-width // HEAD)
    if copies == 1:
        return value[:, :width]
    return jnp.concatenate([value] * copies, axis=1)[:, :width]


def lanes_kernel(out_ref):
    out_ref[...] = rope_lanes()


def pack_kernel(kv_ref, pos_ref, count, rows_ref, out_ref, pos_scratch):
    slots = kv_ref.shape[2]
    pos_scratch[...] = jnp.zeros_like(pos_scratch)
    for group in range(3):
        pos_scratch[group : group + 1, 0:slots] = pos_ref[group].astype(jnp.float32)
    cosine, sine = tables(pos_scratch[...], rows_ref[...])
    cosine, sine = cosine[:slots], sine[:slots]
    slot = lax.broadcasted_iota(jnp.int32, (slots, HEAD), 0)
    lane = lax.broadcasted_iota(jnp.int32, (slots, HEAD), 1)
    live = slot < count[0, 0]
    mark = jnp.where(lane == 0, jnp.inf, 0.0)
    for head in range(HEADS):
        turned = turn(kv_ref[0, 0, :, columns(head)], cosine, sine)
        turned = jnp.where(live, turned, mark if head == 0 else 0.0)
        out_ref[0:slots, columns(head)] = turned.astype(jnp.bfloat16)
    out_ref[slots:, :] = kv_ref[0, 1]


def staged(count, group, first, second, third):
    for base in range(0, count, group):
        steps = range(base, min(base + group, count))
        results = [first(step) for step in steps]
        results = [second(step, result) for step, result in zip(steps, results)]
        results = [third(step, result) for step, result in zip(steps, results)]
        for finish in results:
            finish()


def sums_of(weights, value):
    both = product(weights, jnp.concatenate([value, jnp.ones_like(value)], axis=1), 0)
    return both[:, :HEAD], both[:, HEAD:]


def turn_kernel(order, pairs, *refs):
    query_ref, pair_ref, place_ref, rows_ref, visible_ref = refs[:5]
    rot_ref, key_ref, value_ref, seen_ref = refs[5:9]
    q, k, positions, rows, visible, pos_scratch, sems = refs[9:]
    copies = [
        pltpu.make_async_copy(there, here, sems.at[number])
        for number, (there, here) in enumerate(
            (
                (place_ref, positions),
                (rows_ref, rows),
                (pair_ref.at[0], k),
                (query_ref, q),
                (visible_ref, visible),
                (pair_ref.at[1], value_ref),
            )
        )
    ]
    for copy in copies:
        copy.start()
    tile_rows, wide = q.shape[1], q.shape[2]
    extent = k.shape[1]
    queries, keys = tile_rows * wide, extent * wide
    begin = (extent - tile_rows) // 2 * wide
    pos_scratch[...] = jnp.zeros_like(pos_scratch)
    copies[0].wait()
    for row in range(extent):
        for group in range(3):
            pos_scratch[group : group + 1, row * wide : (row + 1) * wide] = positions[
                group, 0, row : row + 1, :
            ].astype(jnp.float32)
    copies[1].wait()
    cosine, sine = tables(pos_scratch[...], rows[...])
    copies[2].wait()
    for head in range(HEADS):
        part = columns(head)
        key = turn(k[0, :, :, part].reshape(keys, HEAD), cosine, sine)
        key_ref[:, part] = key.astype(jnp.bfloat16)
    cosine, sine = cosine[begin : begin + queries], sine[begin : begin + queries]
    copies[3].wait()
    for head in range(HEADS):
        part = columns(head)
        query = turn(q[0, :, :, part].reshape(queries, HEAD), cosine, sine)
        rot_ref[:, part] = query.astype(jnp.bfloat16)
    copies[4].wait()
    slots = seen_ref.shape[1] // len(order)
    place = lax.broadcasted_iota(jnp.int32, seen_ref.shape, 1) // slots
    seen = jnp.zeros(seen_ref.shape, jnp.int32)
    for number, (offset, cross) in enumerate(order):
        seen = jnp.where(place == number, visible[0, source(offset, cross, pairs)], seen)
    seen_ref[...] = seen
    copies[5].wait()


def local_kernel(masked, *refs):
    rot_ref, key_ref, value_ref, shift_ref, total_ref, sum_ref = refs
    extent, wide = value_ref.shape[1], value_ref.shape[2]
    queries, keys = rot_ref.shape[0], extent * wide
    tile_rows = queries // wide
    reach = (extent - tile_rows) // 2
    if masked:
        tile = lax.axis_index("height")
        count = lax.axis_size("height")
        query_row = lax.broadcasted_iota(jnp.int32, (queries, keys), 0) // wide
        key_row = lax.broadcasted_iota(jnp.int32, (queries, keys), 1) // wide - reach
        first = tile * tile_rows
        allowed = (
            (key_row + first >= 0)
            & (key_row + first < tile_rows * count)
            & (jnp.abs(query_row - key_row) <= REACH)
        )
        cap = jnp.where(allowed, jnp.inf, -jnp.inf)

    def score(head):
        part = columns(head)
        scores = product(rot_ref[:, part], key_ref[:, part], 1)
        return jnp.minimum(scores, cap) if masked else scores

    def weight(head, scores):
        shift = jnp.max(scores, axis=1, keepdims=True) * EXP_SCALE + MARGIN
        shift_ref[:, columns(head)] = jnp.broadcast_to(shift, (queries, HEAD))
        return jnp.exp2(scores * EXP_SCALE - shift).astype(jnp.bfloat16)

    def apply(head, weights):
        part = columns(head)
        sums = sums_of(weights, value_ref[0, :, :, part].reshape(keys, HEAD))

        def store():
            sum_ref[:, part], total_ref[:, part] = sums

        return store

    staged(HEADS, HEADS, score, weight, apply)


def source(offset_own, cross, pairs):
    me = lax.axis_index("tm")
    core = lax.rem(me, 2)
    column = lax.rem(me // 2, 2)
    line = me // 4
    place = jnp.where(column == 0, line, pairs - 1 - line)
    step = jnp.where(core == 0, offset_own, -offset_own)
    there = lax.rem(place - step + 2 * pairs, pairs)
    half = pairs // 2
    far = there >= half
    line = jnp.where(far, pairs - 1 - there, there)
    column = jnp.where(far, 1, 0)
    return line * 4 + column * 2 + (1 - core if cross else core)


def block_kernel(begin, final, *refs):
    rot_ref, shift_ref, total_ref, sum_ref, seen_ref = refs[:5]
    blocks, outs = (refs[5:-1], refs[-1:]) if final else (refs[5:-3], refs[-3:])
    slots = blocks[0].shape[0] // 2
    keys = len(blocks) * slots
    queries = rot_ref.shape[0]
    seen = seen_ref[:, begin * slots : begin * slots + keys]

    def gathered(part, begin):
        return jnp.concatenate([block[begin : begin + slots, part] for block in blocks], axis=0)

    lane = lax.broadcasted_iota(jnp.int32, (8, HEAD), 1)
    pick = jnp.where(lane == 0, 1.0, 0.0).astype(jnp.bfloat16)
    marks = product(pick, gathered(columns(0), 0), 1)
    cap = jnp.where((marks < jnp.inf) & (seen > 0), jnp.inf, -jnp.inf)[0:1]

    def score(part, clean):
        key = gathered(part, 0)
        if clean:
            key = jnp.where(key == jnp.inf, jnp.zeros_like(key), key)
        return jnp.minimum(product(rot_ref[:, part], key, 1), cap)

    def store(part, shift, summed, total):
        if final:
            result = (summed / total).astype(jnp.bfloat16)
            outs[0][0, :, :, part] = result.reshape(outs[0].shape[1], outs[0].shape[2], HEAD)
        else:
            outs[0][:, part] = shift
            outs[1][:, part] = total
            outs[2][:, part] = summed

    top = [jnp.full((8, keys), -jnp.inf)]

    def weight(head, scores):
        power = scores * EXP_SCALE - spread(shift_ref[:, columns(head)], keys)
        top[0] = jnp.maximum(top[0], jnp.max(power.reshape(queries // 8, 8, keys), axis=0))
        return jnp.exp2(power).astype(jnp.bfloat16)

    def apply(head, weights):
        part = columns(head)
        summed, total = sums_of(weights, gathered(part, slots))
        return lambda: store(
            part, shift_ref[:, part], sum_ref[:, part] + summed, total_ref[:, part] + total
        )

    group = HEADS if final else BLOCK_GROUP
    staged(HEADS, group, lambda head: score(columns(head), head == 0), weight, apply)

    @pl.when(jnp.max(top[0]) > 0.0)
    def _():
        @pl.loop(0, HEADS)
        def _(head):
            part = pl.ds(pl.multiple_of(head * HEAD, HEAD), HEAD)
            before = shift_ref[:, part]
            scores = score(part, True)
            shift = jnp.maximum(before, jnp.max(scores, axis=1, keepdims=True) * EXP_SCALE)
            fading = jnp.exp2(before - shift)
            weights = jnp.exp2(scores * EXP_SCALE - spread(shift, keys)).astype(jnp.bfloat16)
            summed, total = sums_of(weights, gathered(part, slots))
            summed, total = sum_ref[:, part] * fading + summed, total_ref[:, part] * fading + total
            store(part, shift, summed, total)


VMEM = pl.BlockSpec(memory_space=pltpu.VMEM)
SMEM = pl.BlockSpec(memory_space=pltpu.SMEM)
HBM = pl.BlockSpec(memory_space=pltpu.HBM)
PARAMS = pltpu.CompilerParams(vmem_limit_bytes=40 * 1024 * 1024)


def cost(flops, size, special):
    return pl.CostEstimate(flops=flops, bytes_accessed=size, transcendentals=special)


def near(array):
    return pltpu.with_memory_space_constraint(array, pltpu.VMEM)


def in_place(array):
    return pltpu.with_memory_space_constraint(array, pltpu.HBM)


def pack(cache_kv, cache_pos, counts):
    slots, depth = cache_kv.shape[2:]
    rows = pl.pallas_call(
        lanes_kernel,
        out_shape=jax.ShapeDtypeStruct((8, HEAD), jnp.float32),
        out_specs=VMEM,
        compiler_params=PARAMS,
        cost_estimate=cost(4000000000, 8000000, 0),
        name="lanes",
    )()
    counts, rows = lax.optimization_barrier((counts, rows))
    return pl.pallas_call(
        pack_kernel,
        out_shape=jax.ShapeDtypeStruct((2 * slots, depth), jnp.bfloat16),
        in_specs=[VMEM, VMEM, SMEM, VMEM],
        out_specs=VMEM,
        scratch_shapes=[pltpu.VMEM((8, 128), jnp.float32)],
        compiler_params=PARAMS,
        name="pack",
    )(cache_kv, cache_pos, counts, rows)


def turn_local(query, pair, pos, rows, visible, order, pairs, slots):
    depth = query.shape[-1]
    queries, keys = query.shape[1] * query.shape[2], pair.shape[2] * pair.shape[3]
    values = pair.shape[1:]
    return pl.pallas_call(
        functools.partial(turn_kernel, order, pairs),
        out_shape=[
            jax.ShapeDtypeStruct((queries, depth), jnp.bfloat16),
            jax.ShapeDtypeStruct((keys, depth), jnp.bfloat16),
            jax.ShapeDtypeStruct(values, jnp.bfloat16),
            jax.ShapeDtypeStruct((8, len(order) * slots), jnp.int32),
        ],
        in_specs=[HBM] * 5,
        out_specs=[VMEM] * 4,
        scratch_shapes=[
            pltpu.VMEM(query.shape, query.dtype),
            pltpu.VMEM(values, pair.dtype),
            pltpu.VMEM(pos.shape, pos.dtype),
            pltpu.VMEM(rows.shape, rows.dtype),
            pltpu.SMEM(visible.shape, visible.dtype),
            pltpu.VMEM((8, keys), jnp.float32),
            pltpu.SemaphoreType.DMA((6,)),
        ],
        compiler_params=PARAMS,
        cost_estimate=cost(0, 4000000, 0),
        name="turn_local",
    )(*[in_place(array) for array in (query, pair, pos, rows, visible)])


def local_attention(rot, key, value, masked):
    queries, depth = rot.shape
    keys = key.shape[0]
    state = jax.ShapeDtypeStruct((queries, depth), jnp.float32)
    return pl.pallas_call(
        functools.partial(local_kernel, masked),
        out_shape=[state] * 3,
        in_specs=[VMEM] * 3,
        out_specs=[VMEM] * 3,
        compiler_params=PARAMS,
        cost_estimate=cost(4 * queries * keys * depth, 4000000, queries * keys * HEADS),
        name="local_attention",
    )(rot, key, value)


def block_attention(rot, state, seen, blocks, begin, out=None):
    queries, depth = rot.shape
    keys = len(blocks) * blocks[0].shape[0] // 2
    final = out is not None
    shape = jax.ShapeDtypeStruct((queries, depth), jnp.float32)
    return pl.pallas_call(
        functools.partial(block_kernel, begin, final),
        out_shape=out if final else [shape] * 3,
        in_specs=[VMEM] * (5 + len(blocks)),
        out_specs=VMEM if final else [VMEM] * 3,
        compiler_params=PARAMS,
        cost_estimate=cost(4 * queries * keys * depth, 9000000, queries * keys * HEADS),
        name="last_attention" if final else "block_attention",
    )(rot, *state, seen, *blocks)


def ring_moves(size, hops=1):
    pairs = size // 2

    def place(index):
        line, column = index // 4, (index // 2) % 2
        return line if column == 0 else pairs - 1 - line

    def index_of(where, core):
        where %= pairs
        column = int(where >= pairs // 2)
        line = pairs - 1 - where if column else where
        return line * 4 + column * 2 + core

    return [
        (index, index_of(place(index) + (hops if index % 2 == 0 else -hops), index % 2))
        for index in range(size)
    ]


def extended(cells, dim, width):
    count = lax.axis_size("height")
    ends = count - 1
    head = lax.slice_in_dim(cells, 0, width, axis=dim)
    tail = lax.slice_in_dim(cells, cells.shape[dim] - width, cells.shape[dim], axis=dim)
    above = lax.ppermute(tail, "height", [(i, i + 1) for i in range(ends)])
    below = lax.ppermute(head, "height", [(i + 1, i) for i in range(ends)])
    return jnp.concatenate([above, cells, below], axis=dim)


def per_device(query, cur_kv, cur_pos, cache_kv, cache_pos, counts, visible):
    size = lax.axis_size("tm")
    pairs = size // 2
    swap = [(index, index ^ 1) for index in range(size)]

    def onward(block, hops=1):
        return lax.ppermute(block, "tm", ring_moves(size, hops))

    def across(block):
        return lax.ppermute(block, "tm", swap)

    rows = jnp.asarray(rope_rows())
    own = pack(cache_kv, jnp.swapaxes(cache_pos, 0, 1), counts)
    masked = lax.axis_size("height") > 1 or query.shape[1] - 1 > REACH
    if lax.axis_size("height") > 1:
        pair, pos = extended(cur_kv, 2, REACH), extended(cur_pos, 2, REACH)
    else:
        pair, pos = cur_kv, cur_pos
    order = [(0, False), (0, True)]
    for step, mixed in ((1, False), (1, True), (3, False), (2, True), (2, False), (4, False), (3, True)):
        order += [(step, mixed), (-step, not mixed)]
    sibling = across(own)
    near_same, near_other = onward(own), onward(sibling)
    rot, key, value, seen = turn_local(
        query, pair, pos, rows, visible, order, pairs, cache_kv.shape[2]
    )
    near_same, rot = lax.optimization_barrier((near_same, rot))
    third = onward(near_same, 2)
    next_other = onward(near_other)
    next_same = onward(near_same)
    shift, *sums = local_attention(rot, key, value, masked)
    third, shift = lax.optimization_barrier((third, shift))
    far = onward(third)
    last = onward(next_other)
    received = (near_same, near_other, third, next_other, next_same, far)
    blocks = [own, sibling] + [block for one in received for block in (one, across(one))]
    last = [last, across(last)]
    state = block_attention(rot, (shift, *sums), seen, blocks, 0)
    out = jax.ShapeDtypeStruct(query.shape, jnp.bfloat16)
    return block_attention(rot, state, seen, last, len(blocks), out)


def solution(mesh):
    in_specs = (
        P(("group", "tm"), "height", None, None),
        P(None, ("group", "tm"), "height", None, None),
        P(None, ("group", "tm"), "height", None),
        P(("group", "tm"), None, "height", None),
        P(("group", "tm"), None, "height"),
        P(("group", "tm"), "height"),
        P(("group", "tm"), None),
    )
    out_specs = P(("group", "tm"), "height", None, None)
    return jax.shard_map(
        per_device, mesh=mesh, in_specs=in_specs, out_specs=out_specs, check_vma=False
    )
```
